32 devices in a mesh: parts: 2 (over x), gx: 16 (over z, y, core).
Axes of the slice: x: 2, y: 2, z: 4, core: 2. Of those that a mesh axis runs over, the one named last changes fastest.
Arguments:
- potential: float32 [512, 32, 1024], P(('parts', 'gx')), parts along dimension 0, may hold values from -15 to 15
- surface_potential: float32 [512, 1024], P(('parts', 'gx')), parts along dimension 0, may hold values from -6 to 6
- elevation: float32 [512, 1024], P(('parts', 'gx')), parts along dimension 0, may hold values from -2.5 to 2.5
- vertical_coeff: float32 [512, 32, 1024], P(('parts', 'gx')), parts along dimension 0, may hold values from 2 to 16
- sigma_slope: float32 [512, 32, 1024], P(('parts', 'gx')), parts along dimension 0, may hold values from -0.8 to 0.8
- inverse_spacing: float32 [512, 1024], P(('parts', 'gx')), parts along dimension 0, may hold values from 0.5 to 2
- wet_tiles: int32 [4, 8], P('parts'), parts along dimension 0, may hold values 0 or 1
- hull_tiles: int32 [4, 8], P('parts'), parts along dimension 0, may hold values 0 or 1
- mooring_nodes: int32 [512], P('parts'), parts along dimension 0, may hold values from 0 to 262143
Outputs:
- new_potential: float32 [512, 32, 1024], P(('parts', 'gx')), parts along dimension 0
- new_elevation: float32 [512, 1024], P(('parts', 'gx')), parts along dimension 0
- new_surface_potential: float32 [512, 1024], P(('parts', 'gx')), parts along dimension 0
- defect_norms: float32 [8], P('parts'), parts along dimension 0
- node_values: float32 [4, 256], P('parts'), parts along dimension 0
The draws below stay inside these ranges and needn't reach their ends.
There are 2 independent parts, one for each index of `parts`. The reference program is written for one: setup_inputs(seed, part) draws one part's arguments, and reference() takes and returns one part's arrays. A program takes and returns all parts, laid end to end along the dimension named above; each array names one. Nothing has to cross between parts.
All inputs are finite; a program needn't handle non-finite values.
Results may differ from the reference program's by a relative error of at most 0.0001.
Values sent between devices are 32-bit elements; how exact they have to be, the bound alone decides.
A program may use at most 128 MiB of HBM per device.

```python
import math
import jax
import jax.numpy as jnp

NY = 1024
NZ = 32
SWEEPS = 4
TILE = 128
NODES = 256
NX = 256


def draw_potential(key, part):
    first_key, second_key = jax.random.split(jax.random.fold_in(key, 7))
    row_pos = jnp.arange(NX, dtype=jnp.float32) / (NX - 1)
    col_exp = jax.random.uniform(second_key, (NY,), jnp.float32, -0.5, 0.5)
    row_scale = 10.0 ** (-0.5 + row_pos)
    base_draw = jnp.clip(jax.random.normal(first_key, (NX, NZ, NY), jnp.float32), -5.0, 5.0)
    return 0.3 * base_draw * row_scale[:, None, None] * (10.0 ** col_exp)[None, None, :]


def set_ends(drawn, key, least, top_value):
    shape = drawn.shape
    index_at = [jax.random.randint(jax.random.fold_in(key, axis), (), 0, shape[axis]) for axis in range(len(shape))]
    drawn = drawn.at[tuple(index_at)].set(least)
    longest = shape.index(max(shape))
    index_at[longest] = (index_at[longest] + 1) % shape[longest]
    return drawn.at[tuple(index_at)].set(top_value)


def shard_levels(own_key, shape, pieces, low, high):
    level, own = 1.0, jax.random.fold_in(own_key, 6)
    for position, parts in pieces:
        steps = jnp.exp(jax.random.uniform(jax.random.fold_in(own, position), (parts,), jnp.float32, low / len(pieces), high / len(pieces)))
        level = level * jnp.repeat(steps, shape[position] // parts).reshape([-1 if axis == position else 1 for axis in range(len(shape))])
    return level


def noise(rng, shape, scale, reach, shards=(), kind=jnp.bfloat16):
    drawn = jax.random.normal(rng, shape, jnp.float32) * scale
    if len(shards) > 0:
        drawn = shard_levels(rng, shape, shards, -0.22, 0.18) * drawn
    return jnp.clip(drawn, min=-reach, max=reach).astype(kind)


def setup_inputs(seed: int = 0, part: int = 0) -> dict:
    seeds = jax.random.split(jax.random.key(seed), 10)
    part_splits = jax.random.split(jax.random.fold_in(seeds[9], part), 10)
    potential = draw_potential(jax.random.fold_in(jax.random.fold_in(seeds[9], part), 71), part)
    surface_potential = noise(part_splits[1], (NX, NY), 1.0, 6.0, ((0, 16),), jnp.float32)
    elevation = noise(part_splits[2], (NX, NY), 0.3, 2.5, ((0, 16),), jnp.float32)
    vertical_coeff = jnp.clip(jnp.exp(math.log(16.0) - 2.0794415 * jax.random.uniform(part_splits[3], (NX, NZ, NY), jnp.float32) ** shard_levels(part_splits[3], (NX, NZ, NY), ((0, 16),), -0.2, 0.2)), 2.0, 16.0)
    sigma_slope = jnp.clip(jax.random.uniform(part_splits[4], (NX, NZ, NY), jnp.float32, -0.8, 0.8) * shard_levels(part_splits[4], (NX, NZ, NY), ((0, 16),), -0.4, 0.0), -0.8, 0.8)
    inverse_spacing = jnp.clip(jnp.exp(math.log(2.0) - 1.3862944 * jax.random.uniform(part_splits[5], (NX, NY), jnp.float32) ** shard_levels(part_splits[5], (NX, NY), ((0, 16),), -0.2, 0.2)), 0.5, 2.0)
    wet_tiles = set_ends((jax.random.randint(part_splits[6], (NX // TILE, NY // TILE), 0, 4) < 3).astype(jnp.int32), jax.random.fold_in(part_splits[6], 1), 0, 1)
    hull_tiles = set_ends((jax.random.randint(part_splits[7], (NX // TILE, NY // TILE), 0, 4) < 1).astype(jnp.int32), jax.random.fold_in(part_splits[7], 1), 0, 1)
    mooring_nodes = set_ends(jax.random.randint(part_splits[8], (NODES,), 0, NX * NY), jax.random.fold_in(part_splits[8], 1), 0, (NX * NY) - 1).astype(jnp.int32)
    return {"potential": potential, "surface_potential": surface_potential, "elevation": elevation, "vertical_coeff": vertical_coeff, "sigma_slope": sigma_slope, "inverse_spacing": inverse_spacing, "wet_tiles": wet_tiles, "hull_tiles": hull_tiles, "mooring_nodes": mooring_nodes}


gravity = 9.81
section_step = 0.05


def defect(padded, surface_ext, coeff_rows, slope_rows):
    stacked_cols = jnp.concatenate([padded, surface_ext[:, None, :]], axis=1)
    vert_diff = stacked_cols[:, 1:] - jnp.concatenate([stacked_cols[:, :1], stacked_cols[:, :-2]], axis=1)
    center = padded[1:-1]
    layer_above = stacked_cols[1:-1, 1:]
    layer_below = jnp.concatenate([center[:, :1], center[:, :-1]], axis=1)
    coeff_below = jnp.concatenate([jnp.zeros_like(coeff_rows[:, :1]), coeff_rows[:, :-1]], axis=1)
    along_x = padded[2:] + padded[:-2] - 2.0 * center
    side_pad = jnp.pad(center, ((0, 0), (0, 0), (1, 1)))
    along_y = side_pad[:, :, 2:] + side_pad[:, :, :-2] - 2.0 * center
    vertical = coeff_rows * (layer_above - center) - coeff_below * (center - layer_below)
    cross_term = 0.25 * slope_rows * (vert_diff[2:] - vert_diff[:-2])
    return along_x + along_y + vertical + cross_term


def column_solve(coeff_rows, right_side):
    layer_count = coeff_rows.shape[1]
    ratio_list = []
    value_list = []
    for layer_no in range(layer_count):
        upper_band = -coeff_rows[:, layer_no]
        if layer_no == 0:
            pivot_value = 4.0 + coeff_rows[:, 0]
            value_now = right_side[:, 0] / pivot_value
        else:
            lower_band = -coeff_rows[:, layer_no - 1]
            pivot_value = 4.0 + coeff_rows[:, layer_no] + coeff_rows[:, layer_no - 1] - lower_band * ratio_list[-1]
            value_now = (right_side[:, layer_no] - lower_band * value_list[-1]) / pivot_value
        ratio_list.append(upper_band / pivot_value)
        value_list.append(value_now)
    solution = [value_list[-1]]
    for layer_no in range(layer_count - 2, -1, -1):
        solution.append(value_list[layer_no] - ratio_list[layer_no] * solution[-1])
    return jnp.stack(solution[::-1], axis=1)


def central(ext_rows, center):
    side_pad = jnp.pad(center, ((0, 0), (1, 1)))
    return (ext_rows[2:] - ext_rows[:-2]) * 0.5, (side_pad[:, 2:] - side_pad[:, :-2]) * 0.5


def surface_step(elev_ext, phis_ext, elevation, surface_potential, top_layer, inverse_spacing, free_mask):
    eta_dx, eta_dy = central(elev_ext, elevation)
    phis_dx, phis_dy = central(phis_ext, surface_potential)
    vertical_speed = (surface_potential - top_layer) * inverse_spacing
    slope_factor = 1.0 + eta_dx * eta_dx + eta_dy * eta_dy
    eta_rate = vertical_speed * slope_factor - (phis_dx * eta_dx + phis_dy * eta_dy)
    phis_rate = -gravity * elevation - 0.5 * (phis_dx * phis_dx + phis_dy * phis_dy - vertical_speed * vertical_speed * slope_factor)
    weight = section_step * free_mask
    return elevation + weight * eta_rate, surface_potential + weight * phis_rate


def reference(potential, surface_potential, elevation, vertical_coeff, sigma_slope, inverse_spacing, wet_tiles, hull_tiles, mooring_nodes):
    potential_now = potential
    phis_pad = jnp.pad(surface_potential, ((1, 1), (0, 0)))
    elev_pad = jnp.pad(elevation, ((1, 1), (0, 0)))
    norm_list = []
    for sweep_no in range(SWEEPS):
        padded = jnp.pad(potential_now, ((1, 1), (0, 0), (0, 0)))
        residual = defect(padded, phis_pad, vertical_coeff, sigma_slope)
        norm_list.append(jnp.sum(residual * residual) / (NX * NZ * NY))
        potential_now = potential_now + column_solve(vertical_coeff, residual)
    tile_mask = (wet_tiles * (1 - hull_tiles)).astype(jnp.float32)
    free_mask = jnp.repeat(jnp.repeat(tile_mask, TILE, axis=0), TILE, axis=1)
    new_elevation, new_surface = surface_step(elev_pad, phis_pad, elevation, surface_potential, potential_now[:, NZ - 1], inverse_spacing, free_mask)
    node_row = mooring_nodes // NY
    node_col = mooring_nodes % NY
    node_values = jnp.stack([new_elevation[node_row, node_col], new_surface[node_row, node_col]])
    return (potential_now, new_elevation, new_surface, jnp.stack(norm_list), node_values)
```

```python
import functools

import jax
import jax.numpy as jnp
from jax import lax
from jax.experimental import pallas as pl
from jax.experimental.pallas import tpu as pltpu
from jax.sharding import PartitionSpec as P

SWEEPS = 4
TILE = 128
SUB = 8
LANE = 128
GRAVITY = 9.81
SECTION_STEP = 0.05
K_UNROLL = 4
MESH = pl.DeviceIdType.MESH


def interior_blocks(rows):
    blocks = []
    start = 2
    while start < rows:
        size = min(7, rows - start)
        blocks.append(list(range(start, start + size)))
        start += size
    return blocks


def side_cells(cells, sub, lane):
    low = pltpu.roll(cells, 1, 1)
    low_wrap = jnp.where(sub == 0, 0.0, pltpu.roll(low, 1, 0))
    high = pltpu.roll(cells, LANE - 1, 1)
    high_wrap = jnp.where(sub == SUB - 1, 0.0, pltpu.roll(high, SUB - 1, 0))
    return (
        jnp.where(lane == 0, low_wrap, low),
        jnp.where(lane == LANE - 1, high_wrap, high),
    )


def kernel(
    count,
    rows,
    layers,
    pot_hbm,
    phis_hbm,
    elev_hbm,
    coeff_hbm,
    slope_hbm,
    spacing_hbm,
    wet_ref,
    hull_ref,
    nodes_ref,
    out_pot,
    out_elev,
    out_phis,
    out_norms,
    out_nodes,
    field,
    coeff,
    slope,
    inverse,
    ratio,
    value,
    spacing,
    new_elev,
    new_phis,
    norm_acc,
    payload,
    gathered,
    edge_sem,
    pot_sem,
    mat_sem,
    spacing_sem,
    out_sem,
    surf_sem,
    send_sem,
    recv_sem,
    all_send,
    all_recv,
):
    me = lax.axis_index("gx")
    last = count - 1
    groups = SUB
    barrier = pltpu.get_barrier_semaphore()

    @pl.loop(1, count)
    def _(t):
        pl.semaphore_signal(
            barrier, inc=1, device_id={"gx": lax.rem(me + t, count)}, device_id_type=MESH
        )

    def cols(j):
        return pl.ds(j * LANE, LANE)

    for j in range(groups):
        for x in (0, rows - 1):
            pltpu.make_async_copy(
                pot_hbm.at[x, :, cols(j)], field.at[0, x + 1, pl.ds(0, layers), j, :], edge_sem.at[0]
            ).start()
        pltpu.make_async_copy(
            phis_hbm.at[:, cols(j)], field.at[0, pl.ds(1, rows), layers, j, :], edge_sem.at[1]
        ).start()
        pltpu.make_async_copy(
            elev_hbm.at[:, cols(j)], field.at[0, pl.ds(1, rows), layers + 1, j, :], edge_sem.at[2]
        ).start()
    for j in range(groups):
        pltpu.make_async_copy(
            pot_hbm.at[pl.ds(1, rows - 2), :, cols(j)],
            field.at[0, pl.ds(2, rows - 2), pl.ds(0, layers), j, :],
            pot_sem,
        ).start()
    half = rows // 2
    for part in range(2):
        for j in range(groups):
            for which, (hbm, buf) in enumerate(((coeff_hbm, coeff), (slope_hbm, slope))):
                pltpu.make_async_copy(
                    hbm.at[pl.ds(part * half, half), :, cols(j)],
                    buf.at[pl.ds(part * half, half), :, j, :],
                    mat_sem.at[part, which],
                ).start()
    for j in range(groups):
        pltpu.make_async_copy(
            spacing_hbm.at[:, cols(j)], spacing.at[:, j, :], spacing_sem
        ).start()

    def wait_bytes(ref, sem):
        pltpu.make_async_copy(ref, ref, sem).wait()

    def wait_mats(part):
        for which, buf in enumerate((coeff, slope)):
            wait_bytes(buf.at[pl.ds(part * half, half)], mat_sem.at[part, which])

    zero = jnp.zeros((SUB, LANE), jnp.float32)

    @pl.when(me == 0)
    def _():
        @pl.loop(0, layers + 2)
        def _(k):
            field[0, 0, k] = zero
            field[1, 0, k] = zero

    @pl.when(me == last)
    def _():
        @pl.loop(0, layers + 2)
        def _(k):
            field[0, rows + 1, k] = zero
            field[1, rows + 1, k] = zero

    def exchange(turn):
        slot = turn % 2
        depth = layers + 2 if turn == 0 else layers
        left = pltpu.make_async_remote_copy(
            src_ref=field.at[slot, 1, pl.ds(0, depth)],
            dst_ref=field.at[slot, rows + 1, pl.ds(0, depth)],
            send_sem=send_sem.at[turn, 0],
            recv_sem=recv_sem.at[turn, 0],
            device_id={"gx": lax.max(me - 1, 0)},
            device_id_type=MESH,
        )
        right = pltpu.make_async_remote_copy(
            src_ref=field.at[slot, rows, pl.ds(0, depth)],
            dst_ref=field.at[slot, 0, pl.ds(0, depth)],
            send_sem=send_sem.at[turn, 1],
            recv_sem=recv_sem.at[turn, 1],
            device_id={"gx": lax.min(me + 1, last)},
            device_id_type=MESH,
        )
        return left, right

    def send(turn):
        left, right = exchange(turn)

        @pl.when(me > 0)
        def _():
            left.start()

        @pl.when(me < last)
        def _():
            right.start()

    def receive(turn):
        left, right = exchange(turn)

        @pl.when(me > 0)
        def _():
            left.wait_send()
            right.wait_recv()

        @pl.when(me < last)
        def _():
            right.wait_send()
            left.wait_recv()

    wait_bytes(pot_hbm.at[pl.ds(0, 2)], edge_sem.at[0])
    wait_bytes(phis_hbm, edge_sem.at[1])
    wait_bytes(elev_hbm, edge_sem.at[2])
    pl.semaphore_wait(barrier, count - 1)
    send(0)

    sub = lax.broadcasted_iota(jnp.int32, (SUB, LANE), 0)
    lane = lax.broadcasted_iota(jnp.int32, (SUB, LANE), 1)

    def forward(sweep, xs):
        src = sweep % 2
        first = sweep == 0
        near = sorted({x + d for x in xs for d in (-1, 0, 1)})

        def body(k, carry):
            now, q_below, q_now, flux_below, term, extra, acc = carry
            above = {x: field[src, x, k + 1] for x in near}
            q_above, flux, terms, extras = [], [], [], []
            for i, x in enumerate(xs):
                at = dict(zip(near, now))
                c = coeff[x - 1, k]
                q = above[x + 1] - above[x - 1]
                f = c * (above[x] - at[x])
                low, high = side_cells(at[x], sub, lane)
                s = slope[x - 1, k]
                if first:
                    s = 0.25 * s
                    slope[x - 1, k] = s
                r = (
                    (at[x + 1] + at[x - 1])
                    + (low + high)
                    - 4.0 * at[x]
                    + (f - flux_below[i])
                    + s * (q - q_below[i])
                )
                acc = acc + r * r
                if first:
                    inv = 1.0 / ((4.0 + c) + extra[i])
                    g = c * inv
                    inverse[x - 1, k] = inv
                    ratio[x - 1, k] = g
                    extras.append(c - c * g)
                else:
                    inv = inverse[x - 1, k]
                v = (r + term[i]) * inv
                value[x - 1, k] = v
                q_above.append(q)
                flux.append(f)
                terms.append(c * v)
            return (
                [above[x] for x in near],
                q_now,
                q_above,
                flux,
                terms,
                extras if first else extra,
                acc,
            )

        now = [field[src, x, 0] for x in near]
        at = dict(zip(near, now))
        q0 = [at[x + 1] - at[x - 1] for x in xs]
        zeros = [zero for _ in xs]
        carry = (now, q0, q0, zeros, zeros, zeros if first else [], zero)
        carry = lax.fori_loop(0, layers, body, carry, unroll=K_UNROLL)
        norm_acc[sweep] += carry[-1]

    def backward(sweep, xs):
        src, dst = sweep % 2, (sweep + 1) % 2

        def body(i, carry):
            k = layers - 1 - i
            out = []
            for u, x in zip(carry, xs):
                u = value[x - 1, k] + ratio[x - 1, k] * u
                field[dst, x, k] = field[src, x, k] + u
                out.append(u)
            return out

        lax.fori_loop(0, layers, body, [zero for _ in xs], unroll=K_UNROLL)

    blocks = interior_blocks(rows)
    edges = [1, rows]
    norm_acc[...] = jnp.zeros_like(norm_acc)

    for sweep in range(SWEEPS):
        final = sweep == SWEEPS - 1
        if sweep == 0:
            wait_bytes(field.at[0, pl.ds(2, rows - 2), pl.ds(0, layers)], pot_sem)
        for number, xs in enumerate(blocks):
            if sweep == 0:
                if number == 0:
                    wait_mats(0)
                if number == 1:
                    wait_mats(1)
            forward(sweep, xs)
            if not final:
                backward(sweep, xs)
        receive(sweep)
        forward(sweep, edges)
        if not final:
            backward(sweep, edges)
            send(sweep + 1)
        if sweep == 0:
            for x in range(rows + 2):
                field[1, x, layers] = field[0, x, layers]

    tile_row = (me * rows) // TILE
    mask = jnp.zeros((SUB, LANE), jnp.int32)
    for j in range(groups):
        free = wet_ref[tile_row, j] * (1 - hull_ref[tile_row, j])
        mask = jnp.where(sub == j, free, mask)
    weight = SECTION_STEP * mask.astype(jnp.float32)
    wait_bytes(spacing, spacing_sem)

    @pl.loop(1, rows + 1)
    def _(x):
        elev = field[0, x, layers + 1]
        phis = field[0, x, layers]
        eta_dx = (field[0, x + 1, layers + 1] - field[0, x - 1, layers + 1]) * 0.5
        phis_dx = (field[0, x + 1, layers] - field[0, x - 1, layers]) * 0.5
        low, high = side_cells(elev, sub, lane)
        eta_dy = (high - low) * 0.5
        low, high = side_cells(phis, sub, lane)
        phis_dy = (high - low) * 0.5
        top = field[SWEEPS % 2 ^ 1, x, layers - 1] + value[x - 1, layers - 1]
        speed = (phis - top) * spacing[x - 1]
        factor = 1.0 + eta_dx * eta_dx + eta_dy * eta_dy
        eta_rate = speed * factor - (phis_dx * eta_dx + phis_dy * eta_dy)
        phis_rate = -GRAVITY * elev - 0.5 * (
            phis_dx * phis_dx + phis_dy * phis_dy - speed * speed * factor
        )
        new_elev[x - 1] = elev + weight * eta_rate
        new_phis[x - 1] = phis + weight * phis_rate

    for j in range(groups):
        for which, (buf, out) in enumerate(((new_elev, out_elev), (new_phis, out_phis))):
            pltpu.make_async_copy(buf.at[:, j, :], out.at[:, cols(j)], surf_sem.at[which]).start()

    local = nodes_ref[...] - me * (rows * groups * LANE)
    node_line = jnp.right_shift(local, 7)
    node_lane = jnp.bitwise_and(local, LANE - 1)
    node_count = local.shape[1]
    lines = rows * groups
    pick_line = (
        lax.broadcasted_iota(jnp.int32, (lines, node_count), 0) == node_line
    ).astype(jnp.float32)
    pick_lane = lax.broadcasted_iota(jnp.int32, (LANE, node_count), 0) == node_lane
    pieces = node_count // LANE
    for which, buf in enumerate((new_elev, new_phis)):
        found = lax.dot_general(
            buf[...].reshape(lines, LANE),
            pick_line,
            (((0,), (0,)), ((), ())),
            precision=lax.Precision.HIGHEST,
            preferred_element_type=jnp.float32,
        )
        found = jnp.sum(jnp.where(pick_lane, found, 0.0), axis=0, keepdims=True)
        for piece in range(pieces):
            line = which * pieces + piece
            payload[line : line + 1, :] = found[:, piece * LANE : (piece + 1) * LANE]
    for sweep in range(SWEEPS):
        line = 2 * pieces + sweep
        payload[line : line + 1, :] = jnp.sum(norm_acc[sweep], axis=0, keepdims=True)
    gathered[me] = payload[...]

    def share(t):
        return pltpu.make_async_remote_copy(
            src_ref=payload,
            dst_ref=gathered.at[me],
            send_sem=all_send.at[t],
            recv_sem=all_recv.at[me],
            device_id={"gx": lax.rem(me + t, count)},
            device_id_type=MESH,
        )

    @pl.loop(1, count)
    def _(t):
        share(t).start()

    for number, xs in enumerate(blocks + [edges]):
        backward(SWEEPS - 1, xs)
        spans = [(xs[0], len(xs))] if xs is not edges else [(x, 1) for x in xs]
        for start, size in spans:
            for j in range(groups):
                pltpu.make_async_copy(
                    field.at[SWEEPS % 2, pl.ds(start, size), pl.ds(0, layers), j, :],
                    out_pot.at[pl.ds(start - 1, size), :, cols(j)],
                    out_sem,
                ).start()

    @pl.loop(1, count)
    def _(t):
        source = lax.rem(me + t, count)
        pltpu.make_async_remote_copy(
            src_ref=payload,
            dst_ref=gathered.at[source],
            send_sem=all_send.at[t],
            recv_sem=all_recv.at[source],
            device_id={"gx": source},
            device_id_type=MESH,
        ).wait()

    total = lax.fori_loop(
        1, count, lambda i, total: total + gathered[i], gathered[0]
    )
    payload[...] = total
    for which in range(2):
        for piece in range(pieces):
            line = which * pieces + piece
            out_nodes[which : which + 1, piece * LANE : (piece + 1) * LANE] = payload[
                line : line + 1, :
            ]
    cells = rows * count * layers * groups * LANE
    for sweep in range(SWEEPS):
        line = 2 * pieces + sweep
        out_norms[sweep] = jnp.sum(payload[line : line + 1, :]) / cells

    for which, (buf, out) in enumerate(((new_elev, out_elev), (new_phis, out_phis))):
        wait_bytes(buf, surf_sem.at[which])
    wait_bytes(field.at[SWEEPS % 2, pl.ds(1, rows), pl.ds(0, layers)], out_sem)


def on_device(
    potential,
    surface_potential,
    elevation,
    vertical_coeff,
    sigma_slope,
    inverse_spacing,
    wet_tiles,
    hull_tiles,
    mooring_nodes,
):
    rows, layers, width = potential.shape
    count = lax.axis_size("gx")
    assert width == SUB * LANE and TILE == LANE and TILE % rows == 0
    node_count = mooring_nodes.shape[0]
    f32 = jnp.float32
    block = (rows, layers, SUB, LANE)
    hbm = pl.BlockSpec(memory_space=pl.ANY)
    smem = pl.BlockSpec(memory_space=pltpu.SMEM)
    vmem = pl.BlockSpec(memory_space=pltpu.VMEM)
    dma = pltpu.SemaphoreType.DMA
    outs = pl.pallas_call(
        functools.partial(kernel, count, rows, layers),
        out_shape=(
            jax.ShapeDtypeStruct(potential.shape, f32),
            jax.ShapeDtypeStruct(elevation.shape, f32),
            jax.ShapeDtypeStruct(elevation.shape, f32),
            jax.ShapeDtypeStruct((SWEEPS,), f32),
            jax.ShapeDtypeStruct((2, node_count), f32),
        ),
        in_specs=[hbm] * 6 + [smem, smem, vmem],
        out_specs=(hbm, hbm, hbm, smem, vmem),
        scratch_shapes=[
            pltpu.VMEM((2, rows + 2, layers + 2, SUB, LANE), f32),
            pltpu.VMEM(block, f32),
            pltpu.VMEM(block, f32),
            pltpu.VMEM(block, f32),
            pltpu.VMEM(block, f32),
            pltpu.VMEM(block, f32),
            pltpu.VMEM((rows, SUB, LANE), f32),
            pltpu.VMEM((rows, SUB, LANE), f32),
            pltpu.VMEM((rows, SUB, LANE), f32),
            pltpu.VMEM((SWEEPS, SUB, LANE), f32),
            pltpu.VMEM((SUB, LANE), f32),
            pltpu.VMEM((count, SUB, LANE), f32),
            dma((3,)),
            dma,
            dma((2, 2)),
            dma,
            dma,
            dma((2,)),
            dma((SWEEPS, 2)),
            dma((SWEEPS, 2)),
            dma((count,)),
            dma((count,)),
        ],
        compiler_params=pltpu.CompilerParams(
            collective_id=0, has_side_effects=True, vmem_limit_bytes=40 * 1024 * 1024
        ),
        name="flow_section",
    )(
        potential,
        surface_potential,
        elevation,
        vertical_coeff,
        sigma_slope,
        inverse_spacing,
        wet_tiles,
        hull_tiles,
        mooring_nodes.reshape(1, node_count),
    )
    return tuple(outs)


def solution(mesh):
    return jax.shard_map(
        on_device,
        mesh=mesh,
        in_specs=(
            P(("parts", "gx"), None, None),
            P(("parts", "gx"), None),
            P(("parts", "gx"), None),
            P(("parts", "gx"), None, None),
            P(("parts", "gx"), None, None),
            P(("parts", "gx"), None),
            P("parts", None),
            P("parts", None),
            P("parts"),
        ),
        out_specs=(
            P(("parts", "gx"), None, None),
            P(("parts", "gx"), None),
            P(("parts", "gx"), None),
            P("parts"),
            P("parts", None),
        ),
        check_vma=False,
    )
```

```python
import functools

import jax
import jax.numpy as jnp
from jax import lax
from jax.experimental import pallas as pl
from jax.experimental.pallas import tpu as pltpu
from jax.sharding import PartitionSpec as P

SWEEPS = 4
TILE = 128
SUB = 8
LANE = 128
GRAVITY = 9.81
SECTION_STEP = 0.05
K_UNROLL = 8
BLOCK_ROWS = 5
VMEM_BYTES = 60 * 1024 * 1024
MESH = pl.DeviceIdType.MESH


def interior_blocks(rows):
    blocks = []
    start = 2
    while start < rows:
        size = min(BLOCK_ROWS, rows - start)
        blocks.append(list(range(start, start + size)))
        start += size
    return blocks


def side_cells(cells, sub, lane):
    low = pltpu.roll(cells, 1, 1)
    low_wrap = jnp.where(sub == 0, 0.0, pltpu.roll(low, 1, 0))
    high = pltpu.roll(cells, LANE - 1, 1)
    high_wrap = jnp.where(sub == SUB - 1, 0.0, pltpu.roll(high, SUB - 1, 0))
    return (
        jnp.where(lane == 0, low_wrap, low),
        jnp.where(lane == LANE - 1, high_wrap, high),
    )


def kernel(
    count,
    rows,
    layers,
    pot_hbm,
    phis_hbm,
    elev_hbm,
    coeff_hbm,
    slope_hbm,
    spacing_hbm,
    wet_hbm,
    hull_hbm,
    nodes_hbm,
    last_pot,
    new_elev,
    new_phis,
    sums,
    field,
    coeff,
    slope,
    inverse,
    ratio,
    value,
    spacing,
    norm_acc,
    payload,
    gathered,
    wet_ref,
    hull_ref,
    nodes_ref,
    small_sem,
    edge_sem,
    pot_sem,
    mat_sem,
    spacing_sem,
    send_sem,
    recv_sem,
    all_send,
    all_recv,
):
    me = lax.axis_index("gx")
    last = count - 1
    groups = SUB
    barrier = pltpu.get_barrier_semaphore()

    @pl.loop(1, count)
    def _(t):
        pl.semaphore_signal(
            barrier, inc=1, device_id={"gx": lax.rem(me + t, count)}, device_id_type=MESH
        )

    def cols(j):
        return pl.ds(j * LANE, LANE)

    for j in range(groups):
        for x in (0, rows - 1):
            pltpu.make_async_copy(
                pot_hbm.at[x, :, cols(j)], field.at[0, x + 1, pl.ds(0, layers), j, :], edge_sem.at[0]
            ).start()
        pltpu.make_async_copy(
            phis_hbm.at[:, cols(j)], field.at[0, pl.ds(1, rows), layers, j, :], edge_sem.at[1]
        ).start()
        pltpu.make_async_copy(
            elev_hbm.at[:, cols(j)], field.at[0, pl.ds(1, rows), layers + 1, j, :], edge_sem.at[2]
        ).start()
    for j in range(groups):
        pltpu.make_async_copy(
            pot_hbm.at[pl.ds(1, rows - 2), :, cols(j)],
            field.at[0, pl.ds(2, rows - 2), pl.ds(0, layers), j, :],
            pot_sem,
        ).start()
    half = rows // 2
    for part in range(2):
        for j in range(groups):
            for which, (hbm, buf) in enumerate(((coeff_hbm, coeff), (slope_hbm, slope))):
                pltpu.make_async_copy(
                    hbm.at[pl.ds(part * half, half), :, cols(j)],
                    buf.at[pl.ds(part * half, half), :, j, :],
                    mat_sem.at[part, which],
                ).start()
    for j in range(groups):
        pltpu.make_async_copy(
            spacing_hbm.at[:, cols(j)], spacing.at[:, j, :], spacing_sem
        ).start()

    small = [
        pltpu.make_async_copy(hbm, buf, small_sem.at[i])
        for i, (hbm, buf) in enumerate(
            ((wet_hbm, wet_ref), (hull_hbm, hull_ref), (nodes_hbm, nodes_ref))
        )
    ]
    for copy in small:
        copy.start()

    def wait_bytes(ref, sem):
        pltpu.make_async_copy(ref, ref, sem).wait()

    def wait_mats(part):
        for which, buf in enumerate((coeff, slope)):
            wait_bytes(buf.at[pl.ds(part * half, half)], mat_sem.at[part, which])

    zero = jnp.zeros((SUB, LANE), jnp.float32)

    @pl.when(me == 0)
    def _():
        @pl.loop(0, layers + 2)
        def _(k):
            field[0, 0, k] = zero
            field[1, 0, k] = zero

    @pl.when(me == last)
    def _():
        @pl.loop(0, layers + 2)
        def _(k):
            field[0, rows + 1, k] = zero
            field[1, rows + 1, k] = zero

    def exchange(turn):
        slot = turn % 2
        depth = layers + 2 if turn == 0 else layers
        left = pltpu.make_async_remote_copy(
            src_ref=field.at[slot, 1, pl.ds(0, depth)],
            dst_ref=field.at[slot, rows + 1, pl.ds(0, depth)],
            send_sem=send_sem.at[turn, 0],
            recv_sem=recv_sem.at[turn, 0],
            device_id={"gx": lax.max(me - 1, 0)},
            device_id_type=MESH,
        )
        right = pltpu.make_async_remote_copy(
            src_ref=field.at[slot, rows, pl.ds(0, depth)],
            dst_ref=field.at[slot, 0, pl.ds(0, depth)],
            send_sem=send_sem.at[turn, 1],
            recv_sem=recv_sem.at[turn, 1],
            device_id={"gx": lax.min(me + 1, last)},
            device_id_type=MESH,
        )
        return left, right

    def send(turn):
        left, right = exchange(turn)

        @pl.when(me > 0)
        def _():
            left.start()

        @pl.when(me < last)
        def _():
            right.start()

    def receive(turn):
        left, right = exchange(turn)

        @pl.when(me > 0)
        def _():
            left.wait_send()
            right.wait_recv()

        @pl.when(me < last)
        def _():
            right.wait_send()
            left.wait_recv()

    wait_bytes(pot_hbm.at[pl.ds(0, 2)], edge_sem.at[0])
    wait_bytes(phis_hbm, edge_sem.at[1])
    wait_bytes(elev_hbm, edge_sem.at[2])
    pl.semaphore_wait(barrier, count - 1)
    send(0)

    sub = lax.broadcasted_iota(jnp.int32, (SUB, LANE), 0)
    lane = lax.broadcasted_iota(jnp.int32, (SUB, LANE), 1)

    def forward(sweep, xs):
        src = sweep % 2
        first = sweep == 0
        near = sorted({x + d for x in xs for d in (-1, 0, 1)})

        def body(k, carry):
            now, sides, q_below, q_now, flux_below, term, extra, acc = carry
            above = {x: field[src, x, k + 1] for x in near}
            q_above, flux, terms, extras, sides_above = [], [], [], [], []
            for i, x in enumerate(xs):
                at = dict(zip(near, now))
                c = coeff[x - 1, k]
                q = above[x + 1] - above[x - 1]
                f = c * (above[x] - at[x])
                low, high = side_cells(above[x], sub, lane)
                sides_above.append(low + high)
                s = slope[x - 1, k]
                if first:
                    s = 0.25 * s
                    slope[x - 1, k] = s
                r = (
                    (at[x + 1] + at[x - 1])
                    + sides[i]
                    - 4.0 * at[x]
                    + (f - flux_below[i])
                    + s * (q - q_below[i])
                )
                acc = acc + r * r
                if first:
                    inv = 1.0 / ((4.0 + c) + extra[i])
                    g = c * inv
                    inverse[x - 1, k] = inv
                    ratio[x - 1, k] = g
                    extras.append(c - c * g)
                else:
                    inv = inverse[x - 1, k]
                    g = ratio[x - 1, k]
                right = r + term[i]
                value[x - 1, k] = right * inv
                q_above.append(q)
                flux.append(f)
                terms.append(right * g)
            return (
                [above[x] for x in near],
                sides_above,
                q_now,
                q_above,
                flux,
                terms,
                extras if first else extra,
                acc,
            )

        now = [field[src, x, 0] for x in near]
        at = dict(zip(near, now))
        q0 = [at[x + 1] - at[x - 1] for x in xs]
        zeros = [zero for _ in xs]
        sides0 = []
        for x in xs:
            low, high = side_cells(at[x], sub, lane)
            sides0.append(low + high)
        carry = (now, sides0, q0, q0, zeros, zeros, zeros if first else [], zero)
        carry = lax.fori_loop(0, layers, body, carry, unroll=K_UNROLL)
        norm_acc[sweep] += carry[-1]

    def backward(sweep, xs):
        src, dst = sweep % 2, (sweep + 1) % 2

        def body(i, carry):
            k = layers - 1 - i
            out = []
            for u, x in zip(carry, xs):
                u = value[x - 1, k] + ratio[x - 1, k] * u
                if sweep == SWEEPS - 1:
                    last_pot[x - 1, k] = field[src, x, k] + u
                else:
                    field[dst, x, k] = field[src, x, k] + u
                out.append(u)
            return out

        lax.fori_loop(0, layers, body, [zero for _ in xs], unroll=K_UNROLL)

    blocks = interior_blocks(rows)
    edges = [1, rows]
    norm_acc[...] = jnp.zeros_like(norm_acc)

    loaded = [False, False]
    for sweep in range(SWEEPS):
        final = sweep == SWEEPS - 1
        if sweep == 0:
            wait_bytes(field.at[0, pl.ds(2, rows - 2), pl.ds(0, layers)], pot_sem)
        for xs in blocks:
            if sweep == 0:
                for part in range(2):
                    if part * half < xs[-1] and not loaded[part]:
                        wait_mats(part)
                        loaded[part] = True
            forward(sweep, xs)
            if not final:
                backward(sweep, xs)
        receive(sweep)
        forward(sweep, edges)
        if not final:
            backward(sweep, edges)
            send(sweep + 1)
        if sweep == 0:
            for x in range(rows + 2):
                field[1, x, layers] = field[0, x, layers]

    for copy in small:
        copy.wait()
    tile_row = (me * rows) // TILE
    mask = jnp.zeros((SUB, LANE), jnp.int32)
    for j in range(groups):
        free = wet_ref[tile_row, j] * (1 - hull_ref[tile_row, j])
        mask = jnp.where(sub == j, free, mask)
    weight = SECTION_STEP * mask.astype(jnp.float32)
    wait_bytes(spacing, spacing_sem)

    @pl.loop(1, rows + 1)
    def _(x):
        elev = field[0, x, layers + 1]
        phis = field[0, x, layers]
        eta_dx = (field[0, x + 1, layers + 1] - field[0, x - 1, layers + 1]) * 0.5
        phis_dx = (field[0, x + 1, layers] - field[0, x - 1, layers]) * 0.5
        low, high = side_cells(elev, sub, lane)
        eta_dy = (high - low) * 0.5
        low, high = side_cells(phis, sub, lane)
        phis_dy = (high - low) * 0.5
        top = field[SWEEPS % 2 ^ 1, x, layers - 1] + value[x - 1, layers - 1]
        speed = (phis - top) * spacing[x - 1]
        factor = 1.0 + eta_dx * eta_dx + eta_dy * eta_dy
        eta_rate = speed * factor - (phis_dx * eta_dx + phis_dy * eta_dy)
        phis_rate = -GRAVITY * elev - 0.5 * (
            phis_dx * phis_dx + phis_dy * phis_dy - speed * speed * factor
        )
        new_elev[x - 1] = elev + weight * eta_rate
        new_phis[x - 1] = phis + weight * phis_rate

    local = nodes_ref[...] - me * (rows * groups * LANE)
    node_line = jnp.right_shift(local, 7)
    node_lane = jnp.bitwise_and(local, LANE - 1)
    node_count = local.shape[1]
    lines = rows * groups
    pick_line = (
        lax.broadcasted_iota(jnp.int32, (lines, node_count), 0) == node_line
    ).astype(jnp.float32)
    pick_lane = lax.broadcasted_iota(jnp.int32, (LANE, node_count), 0) == node_lane
    pieces = node_count // LANE
    for which, buf in enumerate((new_elev, new_phis)):
        found = lax.dot_general(
            buf[...].reshape(lines, LANE),
            pick_line,
            (((0,), (0,)), ((), ())),
            precision=lax.Precision.HIGHEST,
            preferred_element_type=jnp.float32,
        )
        found = jnp.sum(jnp.where(pick_lane, found, 0.0), axis=0, keepdims=True)
        for piece in range(pieces):
            line = which * pieces + piece
            payload[line : line + 1, :] = found[:, piece * LANE : (piece + 1) * LANE]
    for sweep in range(SWEEPS):
        line = 2 * pieces + sweep
        payload[line : line + 1, :] = jnp.sum(norm_acc[sweep], axis=0, keepdims=True)
    gathered[me] = payload[...]

    def share(t):
        return pltpu.make_async_remote_copy(
            src_ref=payload,
            dst_ref=gathered.at[me],
            send_sem=all_send.at[t],
            recv_sem=all_recv.at[me],
            device_id={"gx": lax.rem(me + t, count)},
            device_id_type=MESH,
        )

    @pl.loop(1, count)
    def _(t):
        share(t).start()

    for xs in blocks + [edges]:
        backward(SWEEPS - 1, xs)

    @pl.loop(1, count)
    def _(t):
        source = lax.rem(me + t, count)
        pltpu.make_async_remote_copy(
            src_ref=payload,
            dst_ref=gathered.at[source],
            send_sem=all_send.at[t],
            recv_sem=all_recv.at[source],
            device_id={"gx": source},
            device_id_type=MESH,
        ).wait()

    sums[...] = lax.fori_loop(1, count, lambda i, total: total + gathered[i], gathered[0])


def unpack(
    cells, last_pot, new_elev, new_phis, sums_in, out_pot, out_elev, out_phis, out_norms, out_nodes, sums, sem, sems
):
    small = pltpu.make_async_copy(sums_in, sums, sem)
    small.start()
    copies = []
    for j in range(SUB):
        cols = pl.ds(j * LANE, LANE)
        copies += [
            pltpu.make_async_copy(last_pot.at[:, :, j, :], out_pot.at[:, :, cols], sems.at[0, j]),
            pltpu.make_async_copy(new_elev.at[:, j, :], out_elev.at[:, cols], sems.at[1, j]),
            pltpu.make_async_copy(new_phis.at[:, j, :], out_phis.at[:, cols], sems.at[2, j]),
        ]
    for copy in copies:
        copy.start()
    small.wait()
    pieces = out_nodes.shape[1] // LANE
    for which in range(2):
        for piece in range(pieces):
            line = which * pieces + piece
            out_nodes[which : which + 1, piece * LANE : (piece + 1) * LANE] = sums[
                line : line + 1, :
            ]
    for sweep in range(SWEEPS):
        line = 2 * pieces + sweep
        out_norms[sweep] = jnp.sum(sums[line : line + 1, :]) / cells
    for copy in copies:
        copy.wait()


def on_device(
    potential,
    surface_potential,
    elevation,
    vertical_coeff,
    sigma_slope,
    inverse_spacing,
    wet_tiles,
    hull_tiles,
    mooring_nodes,
):
    rows, layers, width = potential.shape
    count = lax.axis_size("gx")
    assert width == SUB * LANE and TILE == LANE and TILE % rows == 0
    node_count = mooring_nodes.shape[0]
    f32 = jnp.float32
    block = (rows, layers, SUB, LANE)
    hbm = pl.BlockSpec(memory_space=pl.ANY)
    smem = pl.BlockSpec(memory_space=pltpu.SMEM)
    vmem = pl.BlockSpec(memory_space=pltpu.VMEM)
    dma = pltpu.SemaphoreType.DMA
    surface = (rows, SUB, LANE)
    results = pl.pallas_call(
        functools.partial(kernel, count, rows, layers),
        out_shape=(
            pltpu.VMEM(block, f32),
            pltpu.VMEM(surface, f32),
            pltpu.VMEM(surface, f32),
            pltpu.VMEM((SUB, LANE), f32),
        ),
        in_specs=[hbm] * 9,
        out_specs=(vmem,) * 4,
        scratch_shapes=[
            pltpu.VMEM((2, rows + 2, layers + 2, SUB, LANE), f32),
            pltpu.VMEM(block, f32),
            pltpu.VMEM(block, f32),
            pltpu.VMEM(block, f32),
            pltpu.VMEM(block, f32),
            pltpu.VMEM(block, f32),
            pltpu.VMEM(surface, f32),
            pltpu.VMEM((SWEEPS, SUB, LANE), f32),
            pltpu.VMEM((SUB, LANE), f32),
            pltpu.VMEM((count, SUB, LANE), f32),
            pltpu.SMEM(wet_tiles.shape, jnp.int32),
            pltpu.SMEM(hull_tiles.shape, jnp.int32),
            pltpu.VMEM((1, node_count), jnp.int32),
            dma((3,)),
            dma((3,)),
            dma,
            dma((2, 2)),
            dma,
            dma((SWEEPS, 2)),
            dma((SWEEPS, 2)),
            dma((count,)),
            dma((count,)),
        ],
        compiler_params=pltpu.CompilerParams(
            collective_id=0, has_side_effects=True, vmem_limit_bytes=VMEM_BYTES
        ),
        name="flow_section",
    )(
        potential,
        surface_potential,
        elevation,
        vertical_coeff,
        sigma_slope,
        inverse_spacing,
        wet_tiles,
        hull_tiles,
        mooring_nodes.reshape(1, node_count),
    )
    outs = pl.pallas_call(
        functools.partial(unpack, float(rows * count * layers * width)),
        out_shape=(
            jax.ShapeDtypeStruct(potential.shape, f32),
            jax.ShapeDtypeStruct(elevation.shape, f32),
            jax.ShapeDtypeStruct(elevation.shape, f32),
            jax.ShapeDtypeStruct((SWEEPS,), f32),
            jax.ShapeDtypeStruct((2, node_count), f32),
        ),
        in_specs=[hbm] * 4,
        out_specs=(hbm, hbm, hbm, smem, vmem),
        scratch_shapes=[pltpu.VMEM((SUB, LANE), f32), dma, dma((3, SUB))],
        compiler_params=pltpu.CompilerParams(vmem_limit_bytes=8 * 1024 * 1024),
        name="unpack",
    )(*[pltpu.with_memory_space_constraint(r, pltpu.VMEM) for r in results])
    return tuple(outs)


def solution(mesh):
    return jax.shard_map(
        on_device,
        mesh=mesh,
        in_specs=(
            P(("parts", "gx"), None, None),
            P(("parts", "gx"), None),
            P(("parts", "gx"), None),
            P(("parts", "gx"), None, None),
            P(("parts", "gx"), None, None),
            P(("parts", "gx"), None),
            P("parts", None),
            P("parts", None),
            P("parts"),
        ),
        out_specs=(
            P(("parts", "gx"), None, None),
            P(("parts", "gx"), None),
            P(("parts", "gx"), None),
            P("parts"),
            P("parts", None),
        ),
        check_vma=False,
    )
```

```python
import functools

import jax
import jax.numpy as jnp
from jax import lax
from jax.experimental import pallas as pl
from jax.experimental.pallas import tpu as pltpu
from jax.sharding import PartitionSpec as P

SWEEPS = 4
TILE = 128
SUB = 8
LANE = 128
GRAVITY = 9.81
SECTION_STEP = 0.05
K_UNROLL = 8
EDGE_UNROLL = 8
HALVES = 2
BLOCK_ROWS = 5
VMEM_BYTES = 60 * 1024 * 1024
MESH = pl.DeviceIdType.MESH


def interior_blocks(rows):
    blocks = []
    start = 2
    while start < rows:
        size = min(BLOCK_ROWS, rows - start)
        blocks.append(list(range(start, start + size)))
        start += size
    return blocks


def side_cells(cells, sub, lane):
    low = pltpu.roll(cells, 1, 1)
    low_wrap = jnp.where(sub == 0, 0.0, pltpu.roll(low, 1, 0))
    high = pltpu.roll(cells, LANE - 1, 1)
    high_wrap = jnp.where(sub == SUB - 1, 0.0, pltpu.roll(high, SUB - 1, 0))
    return (
        jnp.where(lane == 0, low_wrap, low),
        jnp.where(lane == LANE - 1, high_wrap, high),
    )


def kernel(
    count,
    rows,
    layers,
    pot_hbm,
    phis_hbm,
    elev_hbm,
    coeff_hbm,
    slope_hbm,
    spacing_hbm,
    wet_hbm,
    hull_hbm,
    nodes_hbm,
    last_pot,
    new_elev,
    new_phis,
    sums,
    field,
    coeff,
    slope,
    inverse,
    ratio,
    value,
    spacing,
    norm_acc,
    payload,
    gathered,
    wet_ref,
    hull_ref,
    nodes_ref,
    small_sem,
    edge_sem,
    pot_sem,
    mat_sem,
    spacing_sem,
    send_sem,
    recv_sem,
    all_send,
    all_recv,
):
    me = lax.axis_index("gx")
    last = count - 1
    groups = SUB
    barrier = pltpu.get_barrier_semaphore()

    @pl.loop(1, count)
    def _(t):
        pl.semaphore_signal(
            barrier, inc=1, device_id={"gx": lax.rem(me + t, count)}, device_id_type=MESH
        )

    def cols(j):
        return pl.ds(j * LANE, LANE)

    for j in range(groups):
        for x in (0, rows - 1):
            pltpu.make_async_copy(
                pot_hbm.at[x, :, cols(j)], field.at[0, x + 1, pl.ds(0, layers), j, :], edge_sem.at[0]
            ).start()
        pltpu.make_async_copy(
            phis_hbm.at[:, cols(j)], field.at[0, pl.ds(1, rows), layers, j, :], edge_sem.at[1]
        ).start()
        pltpu.make_async_copy(
            elev_hbm.at[:, cols(j)], field.at[0, pl.ds(1, rows), layers + 1, j, :], edge_sem.at[2]
        ).start()
    for j in range(groups):
        pltpu.make_async_copy(
            pot_hbm.at[pl.ds(1, rows - 2), :, cols(j)],
            field.at[0, pl.ds(2, rows - 2), pl.ds(0, layers), j, :],
            pot_sem,
        ).start()
    half = rows // 2
    for part in range(2):
        for j in range(groups):
            for which, (hbm, buf) in enumerate(((coeff_hbm, coeff), (slope_hbm, slope))):
                pltpu.make_async_copy(
                    hbm.at[pl.ds(part * half, half), :, cols(j)],
                    buf.at[pl.ds(part * half, half), :, j, :],
                    mat_sem.at[part, which],
                ).start()
    for j in range(groups):
        pltpu.make_async_copy(
            spacing_hbm.at[:, cols(j)], spacing.at[:, j, :], spacing_sem
        ).start()

    small = [
        pltpu.make_async_copy(hbm, buf, small_sem.at[i])
        for i, (hbm, buf) in enumerate(
            ((wet_hbm, wet_ref), (hull_hbm, hull_ref), (nodes_hbm, nodes_ref))
        )
    ]
    for copy in small:
        copy.start()

    def wait_bytes(ref, sem):
        pltpu.make_async_copy(ref, ref, sem).wait()

    def wait_mats(part):
        for which, buf in enumerate((coeff, slope)):
            wait_bytes(buf.at[pl.ds(part * half, half)], mat_sem.at[part, which])

    zero = jnp.zeros((SUB, LANE), jnp.float32)

    @pl.when(me == 0)
    def _():
        @pl.loop(0, layers + 2)
        def _(k):
            field[0, 0, k] = zero
            field[1, 0, k] = zero

    @pl.when(me == last)
    def _():
        @pl.loop(0, layers + 2)
        def _(k):
            field[0, rows + 1, k] = zero
            field[1, rows + 1, k] = zero

    def exchange(turn, part):
        lines = pl.ds(part * (SUB // HALVES), SUB // HALVES)
        slot = turn % 2
        depth = layers + 2 if turn == 0 else layers
        left = pltpu.make_async_remote_copy(
            src_ref=field.at[slot, 1, pl.ds(0, depth), lines],
            dst_ref=field.at[slot, rows + 1, pl.ds(0, depth), lines],
            send_sem=send_sem.at[turn, 0, part],
            recv_sem=recv_sem.at[turn, 0, part],
            device_id={"gx": lax.max(me - 1, 0)},
            device_id_type=MESH,
        )
        right = pltpu.make_async_remote_copy(
            src_ref=field.at[slot, rows, pl.ds(0, depth), lines],
            dst_ref=field.at[slot, 0, pl.ds(0, depth), lines],
            send_sem=send_sem.at[turn, 1, part],
            recv_sem=recv_sem.at[turn, 1, part],
            device_id={"gx": lax.min(me + 1, last)},
            device_id_type=MESH,
        )
        return left, right

    def send(turn, part):
        left, right = exchange(turn, part)

        @pl.when(me > 0)
        def _():
            left.start()

        @pl.when(me < last)
        def _():
            right.start()

    def receive(turn, part):
        left, right = exchange(turn, part)

        @pl.when(me > 0)
        def _():
            left.wait_send()
            right.wait_recv()

        @pl.when(me < last)
        def _():
            right.wait_send()
            left.wait_recv()

    wait_bytes(pot_hbm.at[pl.ds(0, 2)], edge_sem.at[0])
    wait_bytes(phis_hbm, edge_sem.at[1])
    wait_bytes(elev_hbm, edge_sem.at[2])
    pl.semaphore_wait(barrier, count - 1)
    for part in range(HALVES):
        send(0, part)

    sub = lax.broadcasted_iota(jnp.int32, (SUB, LANE), 0)
    lane = lax.broadcasted_iota(jnp.int32, (SUB, LANE), 1)

    def forward(sweep, xs):
        src = sweep % 2
        first = sweep == 0
        near = sorted({x + d for x in xs for d in (-1, 0, 1)})

        def body(k, carry):
            now, sides, q_below, q_now, flux_below, term, extra, acc = carry
            above = {x: field[src, x, k + 1] for x in near}
            q_above, flux, terms, extras, sides_above = [], [], [], [], []
            for i, x in enumerate(xs):
                at = dict(zip(near, now))
                c = coeff[x - 1, k]
                q = above[x + 1] - above[x - 1]
                f = c * (above[x] - at[x])
                low, high = side_cells(above[x], sub, lane)
                sides_above.append(low + high)
                s = slope[x - 1, k]
                if first:
                    s = 0.25 * s
                    slope[x - 1, k] = s
                r = (
                    (at[x + 1] + at[x - 1])
                    + sides[i]
                    - 4.0 * at[x]
                    + (f - flux_below[i])
                    + s * (q - q_below[i])
                )
                acc = acc + r * r
                if first:
                    inv = 1.0 / ((4.0 + c) + extra[i])
                    g = c * inv
                    inverse[x - 1, k] = inv
                    ratio[x - 1, k] = g
                    extras.append(c - c * g)
                else:
                    inv = inverse[x - 1, k]
                    g = ratio[x - 1, k]
                right = r + term[i]
                value[x - 1, k] = right * inv
                q_above.append(q)
                flux.append(f)
                terms.append(right * g)
            return (
                [above[x] for x in near],
                sides_above,
                q_now,
                q_above,
                flux,
                terms,
                extras if first else extra,
                acc,
            )

        now = [field[src, x, 0] for x in near]
        at = dict(zip(near, now))
        q0 = [at[x + 1] - at[x - 1] for x in xs]
        zeros = [zero for _ in xs]
        sides0 = []
        for x in xs:
            low, high = side_cells(at[x], sub, lane)
            sides0.append(low + high)
        carry = (now, sides0, q0, q0, zeros, zeros, zeros if first else [], zero)
        carry = lax.fori_loop(0, layers, body, carry, unroll=K_UNROLL)
        norm_acc[sweep] += carry[-1]

    def edge_base(sweep):
        src = sweep % 2

        def body(k, carry):
            now, sides, q_below, q_now, flux_below, extra = carry
            above, sides_above, q_above, flux, extras = [], [], [], [], []
            for i, (x, inner, sign) in enumerate(((1, 2, 1.0), (rows, rows - 1, -1.0))):
                c = coeff[x - 1, k]
                p = field[src, x, k + 1]
                q = sign * field[src, inner, k + 1]
                f = c * (p - now[i])
                low, high = side_cells(p, sub, lane)
                s = slope[x - 1, k]
                if sweep == 0:
                    s = 0.25 * s
                    slope[x - 1, k] = s
                    inv = 1.0 / ((4.0 + c) + extra[i])
                    g = c * inv
                    inverse[x - 1, k] = inv
                    ratio[x - 1, k] = g
                    extras.append(c - c * g)
                value[x - 1, k] = (
                    sign * q_now[i]
                    + sides[i]
                    - 4.0 * now[i]
                    + (f - flux_below[i])
                    + s * (q - q_below[i])
                )
                above.append(p)
                sides_above.append(low + high)
                q_above.append(q)
                flux.append(f)
            return above, sides_above, q_now, q_above, flux, extras

        now = [field[src, x, 0] for x in (1, rows)]
        sides0 = []
        for cells in now:
            low, high = side_cells(cells, sub, lane)
            sides0.append(low + high)
        q0 = [field[src, 2, 0], -field[src, rows - 1, 0]]
        zeros = [zero, zero]
        lax.fori_loop(
            0,
            layers,
            body,
            (now, sides0, q0, q0, zeros, zeros if sweep == 0 else []),
            unroll=K_UNROLL,
        )

    def edge_rows(sweep, part):
        src, dst = sweep % 2, (sweep + 1) % 2
        size = SUB // HALVES
        lines = pl.ds(part * size, size)
        sides = ((1, 0, -1.0), (rows, rows + 1, 1.0))
        empty = jnp.zeros((size, LANE), jnp.float32)

        def down(k, carry):
            h_below, h_now, term, acc = carry
            h_above, terms = [], []
            for i, (x, halo, sign) in enumerate(sides):
                h = field[src, halo, k + 1, lines]
                s = slope[x - 1, k, lines]
                r = (value[x - 1, k, lines] + h_now[i]) + (sign * s) * (h - h_below[i])
                acc = acc + r * r
                right = r + term[i]
                value[x - 1, k, lines] = right * inverse[x - 1, k, lines]
                h_above.append(h)
                terms.append(right * ratio[x - 1, k, lines])
            return h_now, h_above, terms, acc

        h0 = [field[src, halo, 0, lines] for _, halo, _ in sides]
        carry = (h0, h0, [empty, empty], empty)
        carry = lax.fori_loop(0, layers, down, carry, unroll=EDGE_UNROLL)
        norm_acc[sweep, lines] += carry[-1]
        if sweep == SWEEPS - 1:
            return

        def up(i, carry):
            k = layers - 1 - i
            out = []
            for u, (x, _, _) in zip(carry, sides):
                u = value[x - 1, k, lines] + ratio[x - 1, k, lines] * u
                field[dst, x, k, lines] = field[src, x, k, lines] + u
                out.append(u)
            return out

        lax.fori_loop(0, layers, up, [empty, empty], unroll=EDGE_UNROLL)

    def backward(sweep, xs):
        src, dst = sweep % 2, (sweep + 1) % 2

        def body(i, carry):
            k = layers - 1 - i
            out = []
            for u, x in zip(carry, xs):
                u = value[x - 1, k] + ratio[x - 1, k] * u
                if sweep == SWEEPS - 1:
                    last_pot[x - 1, k] = field[src, x, k] + u
                else:
                    field[dst, x, k] = field[src, x, k] + u
                out.append(u)
            return out

        lax.fori_loop(0, layers, body, [zero for _ in xs], unroll=K_UNROLL)

    blocks = interior_blocks(rows)
    edges = [1, rows]
    norm_acc[...] = jnp.zeros_like(norm_acc)

    loaded = [False, False]
    for sweep in range(SWEEPS):
        final = sweep == SWEEPS - 1
        if sweep == 0:
            wait_bytes(field.at[0, pl.ds(2, rows - 2), pl.ds(0, layers)], pot_sem)
        if sweep > 0:
            edge_base(sweep)
        for xs in blocks:
            if sweep == 0:
                for part in range(2):
                    if part * half < xs[-1] and not loaded[part]:
                        wait_mats(part)
                        loaded[part] = True
            forward(sweep, xs)
            if not final:
                backward(sweep, xs)
        if sweep == 0:
            edge_base(0)
        for part in range(HALVES):
            receive(sweep, part)
            edge_rows(sweep, part)
            if not final:
                send(sweep + 1, part)
        if sweep == 0:
            for x in range(rows + 2):
                field[1, x, layers] = field[0, x, layers]

    for copy in small:
        copy.wait()
    tile_row = (me * rows) // TILE
    mask = jnp.zeros((SUB, LANE), jnp.int32)
    for j in range(groups):
        free = wet_ref[tile_row, j] * (1 - hull_ref[tile_row, j])
        mask = jnp.where(sub == j, free, mask)
    weight = SECTION_STEP * mask.astype(jnp.float32)
    wait_bytes(spacing, spacing_sem)

    @pl.loop(1, rows + 1)
    def _(x):
        elev = field[0, x, layers + 1]
        phis = field[0, x, layers]
        eta_dx = (field[0, x + 1, layers + 1] - field[0, x - 1, layers + 1]) * 0.5
        phis_dx = (field[0, x + 1, layers] - field[0, x - 1, layers]) * 0.5
        low, high = side_cells(elev, sub, lane)
        eta_dy = (high - low) * 0.5
        low, high = side_cells(phis, sub, lane)
        phis_dy = (high - low) * 0.5
        top = field[SWEEPS % 2 ^ 1, x, layers - 1] + value[x - 1, layers - 1]
        speed = (phis - top) * spacing[x - 1]
        factor = 1.0 + eta_dx * eta_dx + eta_dy * eta_dy
        eta_rate = speed * factor - (phis_dx * eta_dx + phis_dy * eta_dy)
        phis_rate = -GRAVITY * elev - 0.5 * (
            phis_dx * phis_dx + phis_dy * phis_dy - speed * speed * factor
        )
        new_elev[x - 1] = elev + weight * eta_rate
        new_phis[x - 1] = phis + weight * phis_rate

    local = nodes_ref[...] - me * (rows * groups * LANE)
    node_line = jnp.right_shift(local, 7)
    node_lane = jnp.bitwise_and(local, LANE - 1)
    node_count = local.shape[1]
    lines = rows * groups
    pick_line = (
        lax.broadcasted_iota(jnp.int32, (lines, node_count), 0) == node_line
    ).astype(jnp.float32)
    pick_lane = lax.broadcasted_iota(jnp.int32, (LANE, node_count), 0) == node_lane
    pieces = node_count // LANE
    for which, buf in enumerate((new_elev, new_phis)):
        found = lax.dot_general(
            buf[...].reshape(lines, LANE),
            pick_line,
            (((0,), (0,)), ((), ())),
            precision=lax.Precision.HIGHEST,
            preferred_element_type=jnp.float32,
        )
        found = jnp.sum(jnp.where(pick_lane, found, 0.0), axis=0, keepdims=True)
        for piece in range(pieces):
            line = which * pieces + piece
            payload[line : line + 1, :] = found[:, piece * LANE : (piece + 1) * LANE]
    for sweep in range(SWEEPS):
        line = 2 * pieces + sweep
        payload[line : line + 1, :] = jnp.sum(norm_acc[sweep], axis=0, keepdims=True)
    gathered[me] = payload[...]

    def share(t):
        return pltpu.make_async_remote_copy(
            src_ref=payload,
            dst_ref=gathered.at[me],
            send_sem=all_send.at[t],
            recv_sem=all_recv.at[me],
            device_id={"gx": lax.rem(me + t, count)},
            device_id_type=MESH,
        )

    @pl.loop(1, count)
    def _(t):
        share(t).start()

    for xs in blocks + [edges]:
        backward(SWEEPS - 1, xs)

    @pl.loop(1, count)
    def _(t):
        source = lax.rem(me + t, count)
        pltpu.make_async_remote_copy(
            src_ref=payload,
            dst_ref=gathered.at[source],
            send_sem=all_send.at[t],
            recv_sem=all_recv.at[source],
            device_id={"gx": source},
            device_id_type=MESH,
        ).wait()

    sums[...] = lax.fori_loop(1, count, lambda i, total: total + gathered[i], gathered[0])


def unpack(
    cells, last_pot, new_elev, new_phis, sums_in, out_pot, out_elev, out_phis, out_norms, out_nodes, sums, sem, sems
):
    small = pltpu.make_async_copy(sums_in, sums, sem)
    small.start()
    copies = []
    for j in range(SUB):
        cols = pl.ds(j * LANE, LANE)
        copies += [
            pltpu.make_async_copy(last_pot.at[:, :, j, :], out_pot.at[:, :, cols], sems.at[0, j]),
            pltpu.make_async_copy(new_elev.at[:, j, :], out_elev.at[:, cols], sems.at[1, j]),
            pltpu.make_async_copy(new_phis.at[:, j, :], out_phis.at[:, cols], sems.at[2, j]),
        ]
    for copy in copies:
        copy.start()
    small.wait()
    pieces = out_nodes.shape[1] // LANE
    for which in range(2):
        for piece in range(pieces):
            line = which * pieces + piece
            out_nodes[which : which + 1, piece * LANE : (piece + 1) * LANE] = sums[
                line : line + 1, :
            ]
    for sweep in range(SWEEPS):
        line = 2 * pieces + sweep
        out_norms[sweep] = jnp.sum(sums[line : line + 1, :]) / cells
    for copy in copies:
        copy.wait()


def on_device(
    potential,
    surface_potential,
    elevation,
    vertical_coeff,
    sigma_slope,
    inverse_spacing,
    wet_tiles,
    hull_tiles,
    mooring_nodes,
):
    rows, layers, width = potential.shape
    count = lax.axis_size("gx")
    assert width == SUB * LANE and TILE == LANE and TILE % rows == 0
    node_count = mooring_nodes.shape[0]
    f32 = jnp.float32
    block = (rows, layers, SUB, LANE)
    hbm = pl.BlockSpec(memory_space=pl.ANY)
    smem = pl.BlockSpec(memory_space=pltpu.SMEM)
    vmem = pl.BlockSpec(memory_space=pltpu.VMEM)
    dma = pltpu.SemaphoreType.DMA
    surface = (rows, SUB, LANE)
    results = pl.pallas_call(
        functools.partial(kernel, count, rows, layers),
        out_shape=(
            pltpu.VMEM(block, f32),
            pltpu.VMEM(surface, f32),
            pltpu.VMEM(surface, f32),
            pltpu.VMEM((SUB, LANE), f32),
        ),
        in_specs=[hbm] * 9,
        out_specs=(vmem,) * 4,
        scratch_shapes=[
            pltpu.VMEM((2, rows + 2, layers + 2, SUB, LANE), f32),
            pltpu.VMEM(block, f32),
            pltpu.VMEM(block, f32),
            pltpu.VMEM(block, f32),
            pltpu.VMEM(block, f32),
            pltpu.VMEM(block, f32),
            pltpu.VMEM(surface, f32),
            pltpu.VMEM((SWEEPS, SUB, LANE), f32),
            pltpu.VMEM((SUB, LANE), f32),
            pltpu.VMEM((count, SUB, LANE), f32),
            pltpu.SMEM(wet_tiles.shape, jnp.int32),
            pltpu.SMEM(hull_tiles.shape, jnp.int32),
            pltpu.VMEM((1, node_count), jnp.int32),
            dma((3,)),
            dma((3,)),
            dma,
            dma((2, 2)),
            dma,
            dma((SWEEPS, 2, HALVES)),
            dma((SWEEPS, 2, HALVES)),
            dma((count,)),
            dma((count,)),
        ],
        compiler_params=pltpu.CompilerParams(
            collective_id=0, has_side_effects=True, vmem_limit_bytes=VMEM_BYTES
        ),
        name="flow_section",
    )(
        potential,
        surface_potential,
        elevation,
        vertical_coeff,
        sigma_slope,
        inverse_spacing,
        wet_tiles,
        hull_tiles,
        mooring_nodes.reshape(1, node_count),
    )
    outs = pl.pallas_call(
        functools.partial(unpack, float(rows * count * layers * width)),
        out_shape=(
            jax.ShapeDtypeStruct(potential.shape, f32),
            jax.ShapeDtypeStruct(elevation.shape, f32),
            jax.ShapeDtypeStruct(elevation.shape, f32),
            jax.ShapeDtypeStruct((SWEEPS,), f32),
            jax.ShapeDtypeStruct((2, node_count), f32),
        ),
        in_specs=[hbm] * 4,
        out_specs=(hbm, hbm, hbm, smem, vmem),
        scratch_shapes=[pltpu.VMEM((SUB, LANE), f32), dma, dma((3, SUB))],
        compiler_params=pltpu.CompilerParams(vmem_limit_bytes=8 * 1024 * 1024),
        name="unpack",
    )(*[pltpu.with_memory_space_constraint(r, pltpu.VMEM) for r in results])
    return tuple(outs)


def solution(mesh):
    return jax.shard_map(
        on_device,
        mesh=mesh,
        in_specs=(
            P(("parts", "gx"), None, None),
            P(("parts", "gx"), None),
            P(("parts", "gx"), None),
            P(("parts", "gx"), None, None),
            P(("parts", "gx"), None, None),
            P(("parts", "gx"), None),
            P("parts", None),
            P("parts", None),
            P("parts"),
        ),
        out_specs=(
            P(("parts", "gx"), None, None),
            P(("parts", "gx"), None),
            P(("parts", "gx"), None),
            P("parts"),
            P("parts", None),
        ),
        check_vma=False,
    )
```
